256 devices in a mesh: clip: 4 (over x), seq: 16 (over z, core), split: 4 (over y).
Axes of the slice: x: 4, y: 4, z: 8, core: 2. Of those that a mesh axis runs over, the one named last changes fastest.
Arguments:
- queries: bfloat16 [32768, 4096], P(('clip', 'seq', 'split')), parts along dimension 0, may hold values from -40 to 40
- keys: bfloat16 [32768, 4096], P(('clip', 'seq', 'split')), parts along dimension 0, may hold values from -40 to 40
- values: bfloat16 [32768, 4096], P(('clip', 'seq', 'split')), parts along dimension 0, may hold values from -6 to 6
- key_blocks: int32 [128, 64, 64], P('clip'), parts along dimension 0, may hold values from 0 to 63, as said below
- block_counts: int32 [128, 64], P('clip'), parts along dimension 0, may hold values from 1 to 64, as said below
Outputs:
- attended: bfloat16 [32768, 4096], P(('clip', 'seq', 'split')), parts along dimension 0
The draws below stay inside these ranges and needn't reach their ends.
There are 4 independent parts, one for each index of `clip`. The reference program is written for one: setup_inputs(seed, part) draws one part's arguments, and reference() takes and returns one part's arrays. A program takes and returns all parts, laid end to end along the dimension named above; each array names one. Nothing has to cross between parts.
Inputs may be any that keep to these rules, and one draw needn't show every extreme that they name: `key_blocks`: entry 0 of every list is the query block itself; the entries of one list are distinct; entries past block_counts are not used. `block_counts`: some heads use all 64 entries in every query block.
All inputs are finite; a program needn't handle non-finite values.
Results may differ from the reference program's by a relative error of at most 0.0044.
Values may be sent and summed in bfloat16 or wider, within the bound.
No kernel may reach another device: no remote copies, remote signals or barrier semaphores. Data moves between devices by JAX's collectives and lax.ppermute only.
A program may use at most 128 MiB of HBM per device.

```python
import jax
import jax.numpy as jnp
from jax import lax

HEADS = 32
HEAD_DIM = 128
BLOCK = 128
SEQ_LEN = 8192
KB_MAX = 64


def draw_queries(key, part):
    key = jax.random.fold_in(key, 1)
    result = jnp.clip(jax.random.normal(key, (SEQ_LEN, HEADS * HEAD_DIM), jnp.float32), -4.0, 4.0)
    return result.astype(jnp.bfloat16)


def draw_keys(key, part):
    key = jax.random.fold_in(key, 2)
    result = jnp.clip(jax.random.normal(key, (SEQ_LEN, HEADS * HEAD_DIM), jnp.float32), -4.0, 4.0)
    return result.astype(jnp.bfloat16)


def draw_key_blocks(key, part):
    key = jax.random.fold_in(key, 3)
    blocks = SEQ_LEN // BLOCK
    ranks = jax.random.randint(key, (HEADS, blocks, blocks), 0, 2 ** 20, jnp.int32)
    scores = ranks * blocks + jnp.arange(blocks, dtype=jnp.int32)[None, None, :]
    itself = jnp.arange(blocks)[:, None] == jnp.arange(blocks)[None, :]
    scores = jnp.where(itself[None, :, :], jnp.int32(2 ** 30), scores)
    picked = lax.top_k(scores, KB_MAX)[1]
    return picked.astype(jnp.int32)


def draw_block_counts(key, part):
    key = jax.random.fold_in(key, 5)
    blocks = SEQ_LEN // BLOCK
    first_key, second_key = jax.random.split(key)
    ranking = jax.random.permutation(first_key, HEADS)
    heavy = ranking < HEADS // 4
    light_most = max(2, KB_MAX // 16)
    light = jax.random.randint(second_key, (HEADS, blocks), 1, light_most + 1, jnp.int32)
    return jnp.where(heavy[:, None], jnp.int32(KB_MAX), light).astype(jnp.int32)


def steps_of(stream_key, extent, shards, smallest, high):
    factor_of, own = 1.0, jax.random.fold_in(stream_key, 6)
    for axis_at, blocks in shards:
        heights = jnp.exp(jax.random.uniform(jax.random.fold_in(own, axis_at), (blocks,), jnp.float32, smallest / len(shards), high / len(shards)))
        factor_of = factor_of * jnp.repeat(heights, extent[axis_at] // blocks).reshape([-1 if axis == axis_at else 1 for axis in range(len(extent))])
    return factor_of


def bell_draw(key, extent, spread, most, cuts=(), held_as=jnp.bfloat16):
    gain = steps_of(key, extent, cuts, -0.22, 0.18) if cuts else 1.0
    drawn = jax.random.normal(key, extent, jnp.float32) * spread * gain
    return jnp.minimum(jnp.maximum(drawn, -most), most).astype(held_as)


def setup_inputs(seed: int = 0, part: int = 0) -> dict:
    splits = jax.random.split(jax.random.key(seed), 6)
    part_keys = jax.random.split(jax.random.fold_in(splits[5], part), 6)
    return {
        "queries": draw_queries(jax.random.fold_in(jax.random.fold_in(splits[5], part), 71), part),
        "keys": draw_keys(jax.random.fold_in(jax.random.fold_in(splits[5], part), 71), part),
        "values": bell_draw(part_keys[2], (SEQ_LEN, HEADS * HEAD_DIM), 1.0, 6.0, ((0, 64),)),
        "key_blocks": draw_key_blocks(jax.random.fold_in(jax.random.fold_in(splits[5], part), 71), part),
        "block_counts": draw_block_counts(jax.random.fold_in(jax.random.fold_in(splits[5], part), 71), part),
    }


slot_group = 4


def attend_head(q_blocks, k_head, v_head, lists, counts, scale):
    nrows = q_blocks.shape[0]
    width = q_blocks.shape[1]
    bound = ((jnp.max(counts) + slot_group - 1) // slot_group).astype(jnp.int32)
    q_float = q_blocks.astype(jnp.float32)

    def scored(turn):
        first = (turn * slot_group).astype(jnp.int32)
        picked = lax.dynamic_slice_in_dim(lists, first, slot_group, 1)
        k_group = jnp.take(k_head, picked, axis=0).astype(jnp.float32)
        score = jnp.einsum("qbd,qjkd->qbjk", q_float, k_group) * scale
        slot_ids = first + jnp.arange(slot_group, dtype=jnp.int32)
        usable = slot_ids[None, :] < counts[:, None]
        return jnp.where(usable[:, None, :, None], score, -jnp.inf), picked

    def highest(turn, running):
        score, picked = scored(turn)
        return jnp.maximum(running, jnp.max(score, axis=(2, 3)))

    start = jnp.full((nrows, width), -jnp.inf, jnp.float32)
    running = lax.fori_loop(jnp.int32(0), bound, highest, start)

    def accumulate(turn, carry):
        total, summed = carry
        score, picked = scored(turn)
        expo = jnp.exp(score - running[:, :, None, None])
        v_group = jnp.take(v_head, picked, axis=0).astype(jnp.float32)
        total = total + jnp.sum(expo, axis=(2, 3))
        weight = lax.optimization_barrier(expo.astype(jnp.bfloat16)).astype(jnp.float32)
        summed = summed + jnp.einsum("qbjk,qjkd->qbd", weight, v_group)
        return total, summed

    zero_total = jnp.zeros((nrows, width), jnp.float32)
    zero_summed = jnp.zeros((nrows, width, k_head.shape[2]), jnp.float32)
    total, summed = lax.fori_loop(jnp.int32(0), bound, accumulate, (zero_total, zero_summed))
    return (summed / total[:, :, None]).astype(jnp.bfloat16)


def reference(queries, keys, values, key_blocks, block_counts):
    blocks = SEQ_LEN // BLOCK
    q_four = queries.reshape(blocks, BLOCK, HEADS, HEAD_DIM)
    k_four = keys.reshape(blocks, BLOCK, HEADS, HEAD_DIM)
    v_four = values.reshape(blocks, BLOCK, HEADS, HEAD_DIM)
    scale = HEAD_DIM ** -0.5

    def one_head(head):
        q_head = jnp.take(q_four, head, axis=2)
        k_head = jnp.take(k_four, head, axis=2)
        v_head = jnp.take(v_four, head, axis=2)
        lists = jnp.take(key_blocks, head, axis=0).astype(jnp.int32)
        counts = jnp.take(block_counts, head, axis=0).astype(jnp.int32)
        return attend_head(q_head, k_head, v_head, lists, counts, scale)

    outputs = lax.map(one_head, jnp.arange(HEADS, dtype=jnp.int32))
    return outputs.transpose(1, 2, 0, 3).reshape(SEQ_LEN, HEADS * HEAD_DIM)
```

```python
import functools

import jax
import jax.numpy as jnp
from jax import lax
from jax.experimental import pallas as pl
from jax.experimental.pallas import tpu as pltpu
from jax.sharding import Mesh, PartitionSpec as P

D = 128
BLOCK = 128
GROUP = 4
NEG = -jnp.inf


def col(ref, head):
    return ref[:, pl.ds(pl.multiple_of(head * D, D), D)]


def prep_kernel(tab, q_ref, k_ref, v_ref, *outs):
    n = len(outs) // 3
    for dz in range(n):
        heavy, light, quer = outs[dz], outs[n + dz], outs[2 * n + dz]
        slots = quer.shape[0]
        for s in range(slots):
            head = tab[dz * slots + s]
            quer[s] = col(q_ref, head)
            if s == 0:
                heavy[0] = col(k_ref, head)
                heavy[1] = col(v_ref, head)
            else:
                light[2 * (s - 1)] = col(k_ref, head)
                light[2 * (s - 1) + 1] = col(v_ref, head)


def post_kernel(tab, *refs):
    out = refs[-1]
    n = (len(refs) - 1) // 2
    for dz in range(n):
        heavy, light = refs[dz], refs[n + dz]
        slots = 1 + light.shape[0]
        for s in range(slots):
            head = tab[dz * slots + s]
            data = heavy[0] if s == 0 else light[s - 1]
            out[:, pl.ds(pl.multiple_of(head * D, D), D)] = data


def dot_t(a, b):
    return lax.dot_general(a, b, (((1,), (1,)), ((), ())), preferred_element_type=jnp.float32)


def dot_n(a, b):
    return lax.dot_general(a, b, (((1,), (0,)), ((), ())), preferred_element_type=jnp.float32)


def attend_kernel(first, nh, scale, lists, counts, *refs):
    n = (len(refs) - 3) // 2
    q_refs, kv, outs = refs[:n], refs[n], refs[n + 1 : 2 * n + 1]
    q_all, o_all = refs[2 * n + 1], refs[2 * n + 2]
    members = kv.shape[0]
    per = kv.shape[3]
    total = members * per
    log2e = 1.4426950408889634
    factor = scale * log2e
    for h in range(nh):
        for dz in range(n):
            q_all[dz] = q_refs[dz][first + h]
        low = counts[h * n]
        for dz in range(1, n):
            low = jnp.minimum(low, counts[h * n + dz])

        @pl.when(low == total)
        def dense():
            def part(i, _):
                q = q_all[pl.ds(i * 2, 2)].reshape(2 * BLOCK, D)
                rows = 2 * BLOCK
                m = jnp.full((rows, 1), NEG, jnp.float32)
                l = jnp.zeros((rows, 1), jnp.float32)
                acc = jnp.zeros((rows, D), jnp.float32)
                for g in range(members):
                    k = kv[g, h, 0].reshape(per * BLOCK, D)
                    v = kv[g, h, 1].reshape(per * BLOCK, D)
                    s = dot_t(q, k) * factor
                    new = jnp.maximum(m, jnp.max(s, axis=1, keepdims=True))
                    p = jnp.exp2(s - new)
                    fix = jnp.exp2(m - new)
                    l = l * fix + jnp.sum(p, axis=1, keepdims=True)
                    acc = acc * fix + dot_n(p.astype(jnp.bfloat16), v)
                    m = new
                o_all[pl.ds(i * 2, 2)] = (acc / l).astype(jnp.bfloat16).reshape(2, BLOCK, D)
                return 0

            lax.fori_loop(0, n // 2, part, 0)

        @pl.when(low != total)
        def listed():
            def block_of(pos, which):
                return kv[pos // per, h, which, pos % per]

            def group(q, base, cnt, turn, state):
                m, l, acc = state
                scores = []
                values = []
                for j in range(GROUP):
                    slot = turn * GROUP + j
                    used = slot < cnt
                    pos = lists[base + jnp.where(used, slot, 0)]
                    s = dot_t(q, block_of(pos, 0)) * factor
                    scores.append(jnp.where(used, s, NEG))
                    values.append(block_of(pos, 1))
                s = jnp.concatenate(scores, axis=1)
                v = jnp.concatenate(values, axis=0)
                new = jnp.maximum(m, jnp.max(s, axis=1, keepdims=True))
                p = jnp.exp2(s - new)
                fix = jnp.exp2(m - new)
                l = l * fix + jnp.sum(p, axis=1, keepdims=True)
                acc = acc * fix + dot_n(p.astype(jnp.bfloat16), v)
                return new, l, acc

            wide = 4

            def part(i, _):
                blocks = [i * wide + u for u in range(wide)]
                qs = [q_all[b] for b in blocks]
                cnts = [counts[h * n + b] for b in blocks]
                bases = [(h * n + b) * total for b in blocks]
                start = (
                    jnp.full((BLOCK, 1), NEG, jnp.float32),
                    jnp.zeros((BLOCK, 1), jnp.float32),
                    jnp.zeros((BLOCK, D), jnp.float32),
                )
                states = [group(qs[u], bases[u], cnts[u], 0, start) for u in range(wide)]
                for u in range(wide):
                    more = (cnts[u] + GROUP - 1) // GROUP
                    m, l, acc = lax.fori_loop(
                        1, more, lambda t, st, u=u: group(qs[u], bases[u], cnts[u], t, st), states[u]
                    )
                    o_all[blocks[u]] = (acc / l).astype(jnp.bfloat16)
                return 0

            lax.fori_loop(0, n // wide, part, 0)

        for dz in range(n):
            outs[dz][h] = o_all[dz]


def attend(first, nh, lists, counts, q_parts, kv):
    n = len(q_parts)
    vmem = pl.BlockSpec(memory_space=pltpu.VMEM)
    return pl.pallas_call(
        functools.partial(attend_kernel, first, nh, D ** -0.5),
        out_shape=[jax.ShapeDtypeStruct((nh, BLOCK, D), jnp.bfloat16)] * n,
        grid_spec=pltpu.PrefetchScalarGridSpec(
            num_scalar_prefetch=2,
            grid=(),
            in_specs=[vmem] * (n + 1),
            out_specs=[vmem] * n,
            scratch_shapes=[pltpu.VMEM((n, BLOCK, D), jnp.bfloat16), pltpu.VMEM((n, BLOCK, D), jnp.bfloat16)],
        ),
        compiler_params=pltpu.CompilerParams(vmem_limit_bytes=56 * 2 ** 20),
    )(lists.reshape(-1), counts.reshape(-1), *q_parts, kv)


def body(queries, keys, values, key_blocks, block_counts):
    zs = lax.axis_size("z")
    cores = lax.axis_size("core")
    ys = lax.axis_size("split")
    z, c, y = lax.axis_index("z"), lax.axis_index("core"), lax.axis_index("split")
    heads = queries.shape[1] // D
    slots = heads // zs
    light = slots - 1
    blocks = key_blocks.shape[1]
    members = cores * ys
    vmem = pl.BlockSpec(memory_space=pltpu.VMEM)

    work = jnp.sum(block_counts, axis=1)
    ids = jnp.arange(heads, dtype=jnp.int32)
    ahead = (work[None, :] > work[:, None]) | ((work[None, :] == work[:, None]) & (ids[None, :] < ids[:, None]))
    rank = jnp.sum(ahead.astype(jnp.int32), axis=1)

    def head_at(places):
        return jnp.sum(jnp.where(rank[None, :] == places[:, None], ids[None, :], 0), axis=1)

    spots = jnp.arange(heads, dtype=jnp.int32)
    row = (z + spots // slots) % zs
    slot = spots % slots
    table = head_at(slot * zs + jnp.where(slot % 2 == 0, row, zs - 1 - row))
    mine = table[:slots]

    turn = jnp.arange(zs, dtype=jnp.int32)
    q_ids = ((z - turn) % zs) * members + c * ys + y
    lists = key_blocks[mine[:, None], q_ids[None, :]]
    counts = block_counts[mine[:, None], q_ids[None, :]]
    lists = (lists % members) * zs + (z - lists // members) % zs

    shapes = (
        [jax.ShapeDtypeStruct((2, BLOCK, D), jnp.bfloat16)] * zs
        + [jax.ShapeDtypeStruct((2 * light, BLOCK, D), jnp.bfloat16)] * zs
        + [jax.ShapeDtypeStruct((slots, BLOCK, D), jnp.bfloat16)] * zs
    )
    sent = pl.pallas_call(
        prep_kernel,
        out_shape=shapes,
        grid_spec=pltpu.PrefetchScalarGridSpec(
            num_scalar_prefetch=1, grid=(), in_specs=[vmem] * 3, out_specs=[vmem] * len(shapes)
        ),
        compiler_params=pltpu.CompilerParams(vmem_limit_bytes=56 * 2 ** 20),
    )(table, queries, keys, values)

    def shift(x, k):
        k = k % zs
        if k == 0:
            return x
        return lax.ppermute(x, "z", [(i, (i + k) % zs) for i in range(zs)])

    order = [1, zs - 1, 2, zs - 2, 3, zs - 3, 4, 0]

    def swap(parts, sign):
        got = [None] * zs
        for k in order:
            got[k] = shift(parts[k], sign * k)
        return got

    heavy_kv = swap(sent[:zs], 1)
    light_kv = swap(sent[zs : 2 * zs], 1)
    quer = swap(sent[2 * zs :], 1)

    def gathered(parts, nh):
        x = jnp.stack(parts)
        x = x.transpose(1, 0, 2, 3).reshape(2 * nh * zs * BLOCK, D)
        x = lax.all_gather(x, ("core", "split"), axis=0, tiled=True)
        return x.reshape(members, nh, 2, zs, BLOCK, D)

    heavy_all = gathered(heavy_kv, 1)
    light_all = gathered(light_kv, light)
    heavy_out = attend(0, 1, lists[:1], counts[:1], quer, heavy_all)
    light_out = attend(1, light, lists[1:], counts[1:], quer, light_all)
    heavy_back = swap(heavy_out, -1)
    light_back = swap(light_out, -1)
    return pl.pallas_call(
        post_kernel,
        out_shape=jax.ShapeDtypeStruct(queries.shape, jnp.bfloat16),
        grid_spec=pltpu.PrefetchScalarGridSpec(
            num_scalar_prefetch=1, grid=(), in_specs=[vmem] * (2 * zs), out_specs=vmem
        ),
        compiler_params=pltpu.CompilerParams(vmem_limit_bytes=56 * 2 ** 20),
    )(table, *heavy_back, *light_back)


def solution(mesh):
    clips, seqs, splits = mesh.devices.shape
    fine = Mesh(mesh.devices.reshape(clips, seqs // 2, 2, splits), ("clip", "z", "core", "split"))
    tokens = P(("clip", "z", "core", "split"), None)
    return jax.shard_map(
        body,
        mesh=fine,
        in_specs=(tokens, tokens, tokens, P("clip", None, None), P("clip", None)),
        out_specs=tokens,
        check_vma=False,
    )
```

```python
import functools

import jax
import jax.numpy as jnp
from jax import lax
from jax.experimental import pallas as pl
from jax.experimental.pallas import tpu as pltpu
from jax.sharding import Mesh, PartitionSpec as P

D = 128
BLOCK = 128
GROUP = 4
NEG = -jnp.inf
LOG2E = 1.4426950408889634


def col(ref, head):
    return ref[:, pl.ds(pl.multiple_of(head * D, D), D)]


def prep_kernel(tab, q_ref, k_ref, v_ref, first, second, quer):
    rows, slots = quer.shape[:2]
    near = first.shape[1] // 2
    for r in range(rows):
        for s in range(slots):
            head = tab[r * slots + s]
            ref, i = (first, s) if s < near else (second, s - near)
            ref[r, 2 * i] = col(k_ref, head)
            ref[r, 2 * i + 1] = col(v_ref, head)
            quer[r, s] = col(q_ref, head)


def post_kernel(tab, *refs):
    out = refs[-1]
    slots = sum(x.shape[1] for x in refs[:-1])
    s = 0
    for ref in refs[:-1]:
        for i in range(ref.shape[1]):
            for r in range(ref.shape[0]):
                head = tab[r * slots + s]
                out[:, pl.ds(pl.multiple_of(head * D, D), D)] = ref[r, i]
            s += 1


def dot_t(a, b):
    return lax.dot_general(a, b, (((1,), (1,)), ((), ())), preferred_element_type=jnp.float32)


def dot_n(a, b):
    return lax.dot_general(a, b, (((1,), (0,)), ((), ())), preferred_element_type=jnp.float32)


def soft_step(s, v, state):
    top = jnp.max(s, axis=1, keepdims=True)
    if state is None:
        p = jnp.exp2(s - top)
        return top, jnp.sum(p, axis=1, keepdims=True), dot_n(p.astype(jnp.bfloat16), v)
    m, l, acc = state
    new = jnp.maximum(m, top)
    p = jnp.exp2(s - new)
    fix = jnp.exp2(m - new)
    l = l * fix + jnp.sum(p, axis=1, keepdims=True)
    acc = acc * fix + dot_n(p.astype(jnp.bfloat16), v)
    return new, l, acc


def listed(units, lists, counts, total, factor, q_of, k_of, v_of, put):
    def picked(u, turn):
        spots = []
        for j in range(GROUP):
            slot = turn * GROUP + j
            used = slot < counts[u]
            spots.append((used, lists[u * total + jnp.where(used, slot, 0)]))
        return spots

    def scores(u, spots):
        k = jnp.concatenate([k_of(pos) for _, pos in spots], axis=0)
        s = dot_t(q_of(u), k) * factor
        parts = [jnp.where(used, s[:, j * BLOCK : (j + 1) * BLOCK], NEG) for j, (used, _) in enumerate(spots)]
        return jnp.concatenate(parts, axis=1)

    def vals(spots):
        return jnp.concatenate([v_of(pos) for _, pos in spots], axis=0)

    spots = [picked(u, 0) for u in units]
    s = [scores(u, sp) for u, sp in zip(units, spots)]
    states = [soft_step(x, vals(sp), None) for x, sp in zip(s, spots)]
    for u, state in zip(units, states):
        more = (counts[u] + GROUP - 1) // GROUP

        def step(t, st, u=u):
            sp = picked(u, t)
            return soft_step(scores(u, sp), vals(sp), st)

        _, l, acc = lax.fori_loop(1, more, step, state)
        put(u, (acc / l).astype(jnp.bfloat16))


def attend_head(lists, counts, base, q_of, kv, put):
    members, _, n = kv.shape[:3]
    total = members * n
    factor = D ** -0.5 * LOG2E
    low = counts[base]
    for r in range(1, n):
        low = jnp.minimum(low, counts[base + r])

    @pl.when(low == total)
    def dense():
        wide = n // 2

        def part(i, _):
            q = jnp.concatenate([q_of(i * wide + j) for j in range(wide)], axis=0)
            state = None
            for g in range(members):
                k = kv[g, 0].reshape(n * BLOCK, D)
                v = kv[g, 1].reshape(n * BLOCK, D)
                state = soft_step(dot_t(q, k) * factor, v, state)
            _, l, acc = state
            out = (acc / l).astype(jnp.bfloat16)
            for j in range(wide):
                put(i * wide + j, out[j * BLOCK : (j + 1) * BLOCK])
            return 0

        lax.fori_loop(0, n // wide, part, 0)

    @pl.when(low != total)
    def sparse():
        wide = n // 2

        def part(i, _):
            listed(
                [base + i * wide + j for j in range(wide)], lists, counts, total, factor,
                lambda u: q_of(u - base),
                lambda pos: kv[pos // n, 0, pos % n],
                lambda pos: kv[pos // n, 1, pos % n],
                lambda u, x: put(u - base, x),
            )
            return 0

        lax.fori_loop(0, n // wide, part, 0)


def near_kernel(slot, lists, counts, own, other, q_ref, o_ref, kv, sems):
    half = own.shape[0]
    copies = [
        pltpu.make_async_copy(own, kv.at[pl.ds(0, half)], sems.at[0]),
        pltpu.make_async_copy(other, kv.at[pl.ds(half, half)], sems.at[1]),
    ]
    for copy in copies:
        copy.start()
    for copy in copies:
        copy.wait()

    def put(r, x):
        o_ref[r, 0] = x

    attend_head(lists, counts, 0, lambda r: q_ref[r, slot], kv, put)


def gathered_kernel(skip, lists, counts, q_ref, kv, o_ref):
    n = q_ref.shape[0]
    h = pl.program_id(0)

    def put(r, x):
        o_ref[r, 0] = x

    attend_head(lists, counts, h * n, lambda r: q_ref[r, skip + h], kv.at[:, 0], put)


def local_call(kernel, scalars, inputs, shapes, scratch=(), hbm=0):
    vmem = pl.BlockSpec(memory_space=pltpu.VMEM)
    anywhere = pl.BlockSpec(memory_space=pl.ANY)
    return pl.pallas_call(
        kernel,
        out_shape=[jax.ShapeDtypeStruct(x, jnp.bfloat16) for x in shapes],
        grid_spec=pltpu.PrefetchScalarGridSpec(
            num_scalar_prefetch=len(scalars),
            grid=(),
            in_specs=[anywhere] * hbm + [vmem] * (len(inputs) - hbm),
            out_specs=[vmem] * len(shapes),
            scratch_shapes=list(scratch),
        ),
        compiler_params=pltpu.CompilerParams(vmem_limit_bytes=56 * 2 ** 20),
    )(*scalars, *inputs)


def body(queries, keys, values, key_blocks, block_counts):
    zs = lax.axis_size("z")
    cores = lax.axis_size("core")
    ys = lax.axis_size("split")
    z, c, y = lax.axis_index("z"), lax.axis_index("core"), lax.axis_index("split")
    heads = queries.shape[1] // D
    blocks = key_blocks.shape[1]
    members = cores * ys
    slots = heads // zs

    work = jnp.sum(block_counts, axis=1)
    ids = jnp.arange(heads, dtype=jnp.int32)
    ahead = (work[None, :] > work[:, None]) | ((work[None, :] == work[:, None]) & (ids[None, :] < ids[:, None]))
    rank = jnp.sum(ahead.astype(jnp.int32), axis=1)

    def head_at(places):
        return jnp.sum(jnp.where(rank[None, :] == places[:, None], ids[None, :], 0), axis=1)

    spots = jnp.arange(heads, dtype=jnp.int32)
    row, slot = spots // slots, spots % slots
    table = head_at(slot * zs + jnp.where(slot % 2 == 0, row, zs - 1 - row))
    mine = lax.dynamic_slice_in_dim(table, z * slots, slots)

    q_ids = jnp.arange(zs, dtype=jnp.int32) * members + c * ys + y
    lists = key_blocks[mine[:, None], q_ids[None, :]]
    counts = block_counts[mine[:, None], q_ids[None, :]]
    lz, lc, ly = lists // members, lists // ys % cores, lists % ys
    near = (jnp.arange(slots) == 1)[:, None, None]
    lists = jnp.where(near, (lc + c) % cores * ys + (y - ly) % ys, lc * ys + ly) * zs + lz

    first, second, quer = local_call(
        prep_kernel, [table], [queries, keys, values],
        [(zs, 4, BLOCK, D), (zs, 2 * (slots - 2), BLOCK, D), (zs, slots, BLOCK, D)],
    )

    def swap(x):
        return lax.all_to_all(x, "z", split_axis=0, concat_axis=0, tiled=True)

    def packed(x):
        return x.transpose(1, 0, 2, 3).reshape(-1, D)

    def gathered(x):
        nh = x.shape[0] // (2 * zs * BLOCK)
        x = lax.all_gather(x, ("core", "split"), axis=0, tiled=True)
        return x.reshape(members, nh, 2, zs, BLOCK, D)

    first = swap(first)
    wide_kv, near_kv = packed(first[:, :2]), first[:, 2:].transpose(1, 0, 2, 3)
    wide_kv, near_kv, second = lax.optimization_barrier((wide_kv, near_kv, second))
    wide_kv = gathered(wide_kv)
    near_parts = [near_kv]
    for dy in range(1, ys):
        near_parts.append(lax.ppermute(near_kv, "split", [(i, (i + dy) % ys) for i in range(ys)]))
    second, quer = lax.optimization_barrier((packed(swap(second)), quer))
    light_kv = gathered(second)
    quer, lists, counts = lax.optimization_barrier((swap(quer), lists, counts))

    def attend(slot, kv):
        nh = kv.shape[1]
        return pl.pallas_call(
            functools.partial(gathered_kernel, slot),
            out_shape=jax.ShapeDtypeStruct((zs, nh, BLOCK, D), jnp.bfloat16),
            grid_spec=pltpu.PrefetchScalarGridSpec(
                num_scalar_prefetch=2,
                grid=(nh,),
                in_specs=[
                    pl.BlockSpec(quer.shape, lambda h, *_: (0, 0, 0, 0)),
                    pl.BlockSpec((members, 1, 2, zs, BLOCK, D), lambda h, *_: (0, h, 0, 0, 0, 0)),
                ],
                out_specs=pl.BlockSpec((zs, 1, BLOCK, D), lambda h, *_: (0, h, 0, 0)),
            ),
            compiler_params=pltpu.CompilerParams(vmem_limit_bytes=56 * 2 ** 20),
        )(lists[slot : slot + nh].reshape(-1), counts[slot : slot + nh].reshape(-1), quer, kv)

    wide_out = attend(0, wide_kv)
    near_parts, wide_out = lax.optimization_barrier((near_parts, wide_out))
    near_kv = jnp.stack(near_parts)
    other_kv = lax.ppermute(near_kv, "core", [(0, 1), (1, 0)])
    near_out = local_call(
        functools.partial(near_kernel, 1), [lists[1].reshape(-1), counts[1]],
        [near_kv, other_kv, quer], [(zs, 1, BLOCK, D)],
        [pltpu.VMEM((members, 2, zs, BLOCK, D), jnp.bfloat16), pltpu.SemaphoreType.DMA((2,))],
        hbm=2,
    )[0]
    early_out = swap(wide_out)
    late_out = swap(jnp.concatenate([near_out, attend(2, light_kv)], axis=1))
    return local_call(post_kernel, [table], [early_out, late_out], [queries.shape])[0]


def solution(mesh):
    clips, seqs, splits = mesh.devices.shape
    fine = Mesh(mesh.devices.reshape(clips, seqs // 2, 2, splits), ("clip", "z", "core", "split"))
    tokens = P(("clip", "z", "core", "split"), None)
    return jax.shard_map(
        body,
        mesh=fine,
        in_specs=(tokens, tokens, tokens, P("clip", None, None), P("clip", None)),
        out_specs=tokens,
        check_vma=False,
    )
```

```python
import functools

import jax
import jax.numpy as jnp
from jax import lax
from jax.experimental import pallas as pl
from jax.experimental.pallas import tpu as pltpu
from jax.sharding import Mesh, PartitionSpec as P

D = 128
BLOCK = 128
GROUP = 4
NEG = -jnp.inf
LOG2E = 1.4426950408889634


def col(ref, head):
    return ref[:, pl.ds(pl.multiple_of(head * D, D), D)]


def wide_prep(tab, q_ref, k_ref, v_ref, wide):
    for r in range(wide.shape[0]):
        for i, ref in enumerate((q_ref, k_ref, v_ref)):
            wide[r, i] = col(ref, tab[r])


def light_prep(rows, tab, q_ref, k_ref, v_ref, light):
    columns = light.shape[0] // rows
    used = tab.shape[0] // rows - 1
    for r in range(rows):
        for y in range(used):
            head = tab[rows + r * used + y]
            for i, ref in enumerate((q_ref, k_ref, v_ref)):
                light[r * columns + y, i] = col(ref, head)


def post_kernel(rows, tab, light, out):
    columns = light.shape[0] // rows
    used = tab.shape[0] // rows - 1
    for r in range(rows):
        out[:, pl.ds(pl.multiple_of(tab[r] * D, D), D)] = light[r * columns + used]
        for y in range(used):
            at = pl.ds(pl.multiple_of(tab[rows + r * used + y] * D, D), D)
            out[:, at] = light[r * columns + y]


def dot_t(a, b):
    return lax.dot_general(a, b, (((1,), (1,)), ((), ())), preferred_element_type=jnp.float32)


def dot_n(a, b):
    return lax.dot_general(a, b, (((1,), (0,)), ((), ())), preferred_element_type=jnp.float32)


def soft_step(s, v, state):
    top = jnp.max(s, axis=1, keepdims=True)
    if state is None:
        p = jnp.exp2(s - top)
        return top, jnp.sum(p, axis=1, keepdims=True), dot_n(p.astype(jnp.bfloat16), v)
    m, l, acc = state
    new = jnp.maximum(m, top)
    p = jnp.exp2(s - new)
    fix = jnp.exp2(m - new)
    l = l * fix + jnp.sum(p, axis=1, keepdims=True)
    acc = acc * fix + dot_n(p.astype(jnp.bfloat16), v)
    return new, l, acc


def listed(units, lists, counts, total, factor, q_of, k_of, v_of, put):
    def picked(u, turn):
        spots = []
        for j in range(GROUP):
            slot = turn * GROUP + j
            used = slot < counts[u]
            spots.append((used, lists[u * total + jnp.where(used, slot, 0)]))
        return spots

    def scores(u, spots):
        k = jnp.concatenate([k_of(pos) for _, pos in spots], axis=0)
        s = dot_t(q_of(u), k) * factor
        parts = [jnp.where(used, s[:, j * BLOCK : (j + 1) * BLOCK], NEG) for j, (used, _) in enumerate(spots)]
        return jnp.concatenate(parts, axis=1)

    def vals(spots):
        return jnp.concatenate([v_of(pos) for _, pos in spots], axis=0)

    spots = [picked(u, 0) for u in units]
    s = [scores(u, sp) for u, sp in zip(units, spots)]
    states = [soft_step(x, vals(sp), None) for x, sp in zip(s, spots)]
    for u, state in zip(units, states):
        more = (counts[u] + GROUP - 1) // GROUP

        def step(t, st, u=u):
            sp = picked(u, t)
            return soft_step(scores(u, sp), vals(sp), st)

        _, l, acc = lax.fori_loop(1, more, step, state)
        put(u, (acc / l).astype(jnp.bfloat16))


def attend_head(lists, counts, base, q_of, kv, put):
    members, _, n = kv.shape[:3]
    total = members * n
    factor = D ** -0.5 * LOG2E
    low = counts[base]
    for r in range(1, n):
        low = jnp.minimum(low, counts[base + r])

    @pl.when(low == total)
    def dense():
        wide = n // 2

        def part(i, _):
            q = jnp.concatenate([q_of(i * wide + j) for j in range(wide)], axis=0)
            state = None
            for g in range(members):
                k = kv[g, 0].reshape(n * BLOCK, D)
                v = kv[g, 1].reshape(n * BLOCK, D)
                state = soft_step(dot_t(q, k) * factor, v, state)
            _, l, acc = state
            out = (acc / l).astype(jnp.bfloat16)
            for j in range(wide):
                put(i * wide + j, out[j * BLOCK : (j + 1) * BLOCK])
            return 0

        lax.fori_loop(0, n // wide, part, 0)

    @pl.when(low != total)
    def sparse():
        wide = n // 2

        def part(i, _):
            listed(
                [base + i * wide + j for j in range(wide)], lists, counts, total, factor,
                lambda u: q_of(u - base),
                lambda pos: kv[pos // n, 0, pos % n],
                lambda pos: kv[pos // n, 1, pos % n],
                lambda u, x: put(u - base, x),
            )
            return 0

        lax.fori_loop(0, n // wide, part, 0)


def wide_kernel(lists, counts, *refs):
    parts, (q_ref, o_ref, kv, sems) = refs[:-4], refs[-4:]
    copies = [pltpu.make_async_copy(part, kv.at[i], sems.at[i]) for i, part in enumerate(parts)]
    for copy in copies:
        copy.start()
    for copy in copies:
        copy.wait()

    def put(r, x):
        o_ref[r] = x

    attend_head(lists, counts, 0, lambda r: q_ref[r], kv, put)


def hand_on_kernel(counts, *refs):
    passed, (_, out, sems) = refs[:-3], refs[-3:]

    @pl.when(counts[0] == 0)
    def place():
        copies = [pltpu.make_async_copy(ref, out.at[:, y], sems.at[y]) for y, ref in enumerate(passed)]
        for copy in copies:
            copy.start()
        for copy in copies:
            copy.wait()


def light_kernel(total, lists, counts, own, other, o_ref, q_ref, kv, sems):
    units = q_ref.shape[0]

    @pl.when(counts[0] > 0)
    def work():
        copies = [
            pltpu.make_async_copy(own.at[:, 0], q_ref, sems.at[0]),
            pltpu.make_async_copy(own.at[:, 1:], kv.at[pl.ds(0, units)], sems.at[1]),
            pltpu.make_async_copy(other.at[:, 1:], kv.at[pl.ds(units, units)], sems.at[2]),
        ]
        for copy in copies:
            copy.start()
        for copy in copies:
            copy.wait()

        def put(u, x):
            o_ref[u] = x

        wide = 16

        def some(i, _):
            listed(
                [i * wide + j for j in range(wide)], lists, counts, total, D ** -0.5 * LOG2E,
                lambda u: q_ref[u], lambda pos: kv[pos, 0], lambda pos: kv[pos, 1], put,
            )
            return 0

        lax.fori_loop(0, units // wide, some, 0)


def local_call(kernel, scalars, inputs, shapes, scratch=(), hbm=0):
    vmem = pl.BlockSpec(memory_space=pltpu.VMEM)
    anywhere = pl.BlockSpec(memory_space=pl.ANY)
    return pl.pallas_call(
        kernel,
        out_shape=[jax.ShapeDtypeStruct(x, jnp.bfloat16) for x in shapes],
        grid_spec=pltpu.PrefetchScalarGridSpec(
            num_scalar_prefetch=len(scalars),
            grid=(),
            in_specs=[anywhere] * hbm + [vmem] * (len(inputs) - hbm),
            out_specs=[vmem] * len(shapes),
            scratch_shapes=list(scratch),
        ),
        compiler_params=pltpu.CompilerParams(vmem_limit_bytes=56 * 2 ** 20),
    )(*scalars, *inputs)


def body(queries, keys, values, key_blocks, block_counts):
    zs = lax.axis_size("z")
    cores = lax.axis_size("core")
    ys = lax.axis_size("split")
    z, c, y = lax.axis_index("z"), lax.axis_index("core"), lax.axis_index("split")
    heads = queries.shape[1] // D
    blocks = key_blocks.shape[1]
    members = cores * ys

    work = jnp.sum(block_counts, axis=1)
    ids = jnp.arange(heads, dtype=jnp.int32)
    ahead = (work[None, :] > work[:, None]) | ((work[None, :] == work[:, None]) & (ids[None, :] < ids[:, None]))
    rank = jnp.sum(ahead.astype(jnp.int32), axis=1)

    def head_at(places):
        return jnp.sum(jnp.where(rank[None, :] == places[:, None], ids[None, :], 0), axis=1)

    used = heads // zs - 1
    rows = jnp.arange(zs, dtype=jnp.int32)
    columns = jnp.arange(used, dtype=jnp.int32)
    table = head_at(jnp.concatenate([rows, ((1 + columns)[None, :] * zs + rows[:, None]).reshape(-1)]))

    def places(lists):
        return lists // members, lists // ys % cores, lists % ys

    wide_head = lax.dynamic_index_in_dim(table, z, keepdims=False)
    wide_ids = rows * members + c * ys + y
    wide_counts = block_counts[wide_head][wide_ids]
    lz, lc, ly = places(key_blocks[wide_head][wide_ids])
    wide_lists = ((lc + c) % cores * ys + (y - ly) % ys) * zs + lz
    light_head = lax.dynamic_index_in_dim(table, zs + z * used + jnp.minimum(y, used - 1), keepdims=False)
    light_ids = jnp.arange(zs * ys, dtype=jnp.int32)
    light_ids = light_ids // ys * members + c * ys + light_ids % ys
    light_counts = jnp.where(y < used, block_counts[light_head][light_ids], 0)
    lz, lc, ly = places(key_blocks[light_head][light_ids])
    light_lists = (lc + c) % cores * (zs * ys) + lz * ys + ly

    wide = local_call(wide_prep, [table], [queries, keys, values], [(zs, 3, BLOCK, D)])[0]
    light = local_call(
        functools.partial(light_prep, zs), [table], [queries, keys, values], [(zs * ys, 3, BLOCK, D)]
    )[0]

    def spread(x):
        return lax.all_to_all(x, ("z", "split"), split_axis=0, concat_axis=0, tiled=True)

    def over_cores(x):
        return lax.ppermute(x, "core", [(0, 1), (1, 0)])

    wide = lax.all_to_all(wide, "z", split_axis=0, concat_axis=0, tiled=True)
    wide, wide_lists, wide_counts, light_lists, light_counts = lax.optimization_barrier(
        (wide, wide_lists, wide_counts, light_lists, light_counts)
    )
    wide_q, wide_kv = wide[:, 0], wide[:, 1:].transpose(1, 0, 2, 3)
    wide_q, wide_kv, light = lax.optimization_barrier((wide_q, wide_kv, light))
    parts = [wide_kv]
    for dy in range(1, ys):
        parts.append(lax.ppermute(wide_kv, "split", [(i, (i + dy) % ys) for i in range(ys)]))
    parts = parts + [over_cores(x) for x in parts]
    light = spread(light)
    wide_out = local_call(
        wide_kernel, [wide_lists.reshape(-1), wide_counts], [*parts, wide_q], [(zs, BLOCK, D)],
        [pltpu.VMEM((members, 2, zs, BLOCK, D), jnp.bfloat16), pltpu.SemaphoreType.DMA((members,))],
        hbm=members,
    )[0]
    light, wide_out = lax.optimization_barrier((light, wide_out))
    light_out = local_call(
        functools.partial(light_kernel, blocks), [light_lists.reshape(-1), light_counts],
        [light, over_cores(light)], [(zs * ys, BLOCK, D)],
        [
            pltpu.VMEM((zs * ys, BLOCK, D), jnp.bfloat16),
            pltpu.VMEM((blocks, 2, BLOCK, D), jnp.bfloat16),
            pltpu.SemaphoreType.DMA((3,)),
        ],
        hbm=2,
    )[0]
    passed = [lax.ppermute(wide_out, "split", [(i, used)]) for i in range(used)] + [wide_out]
    anywhere = pl.BlockSpec(memory_space=pl.ANY)
    light_out = pl.pallas_call(
        hand_on_kernel,
        out_shape=jax.ShapeDtypeStruct((zs, ys, BLOCK, D), jnp.bfloat16),
        grid_spec=pltpu.PrefetchScalarGridSpec(
            num_scalar_prefetch=1,
            grid=(),
            in_specs=[pl.BlockSpec(memory_space=pltpu.VMEM)] * ys + [anywhere],
            out_specs=anywhere,
            scratch_shapes=[pltpu.SemaphoreType.DMA((ys,))],
        ),
        input_output_aliases={ys + 1: 0},
    )(light_counts, *passed, light_out.reshape(zs, ys, BLOCK, D))
    light_out = spread(light_out.reshape(zs * ys, BLOCK, D))
    return local_call(functools.partial(post_kernel, zs), [table], [light_out], [queries.shape])[0]


def solution(mesh):
    clips, seqs, splits = mesh.devices.shape
    fine = Mesh(mesh.devices.reshape(clips, seqs // 2, 2, splits), ("clip", "z", "core", "split"))
    tokens = P(("clip", "z", "core", "split"), None)
    return jax.shard_map(
        body,
        mesh=fine,
        in_specs=(tokens, tokens, tokens, P("clip", None, None), P("clip", None)),
        out_specs=tokens,
        check_vma=False,
    )
```

```python
import functools

import jax
import jax.numpy as jnp
from jax import lax
from jax.experimental import pallas as pl
from jax.experimental.pallas import tpu as pltpu
from jax.sharding import Mesh, PartitionSpec as P

D = 128
BLOCK = 128
GROUP = 4
NEG = -jnp.inf
LOG2E = 1.4426950408889634


def col(ref, head):
    return ref[:, pl.ds(pl.multiple_of(head * D, D), D)]


def wide_prep(tab, q_ref, k_ref, v_ref, wide, sems):
    copies = []
    for r in range(wide.shape[0]):
        at = pl.ds(pl.multiple_of(tab[r] * D, D), D)
        for i, ref in enumerate((q_ref, k_ref, v_ref)):
            copies.append(pltpu.make_async_copy(ref.at[:, at], wide.at[r, i], sems.at[r, i]))
    for copy in copies:
        copy.start()
    for copy in copies:
        copy.wait()


def light_prep(rows, tab, q_ref, k_ref, v_ref, light):
    columns = light.shape[0] // rows
    used = tab.shape[0] // rows - 1
    for r in range(rows):
        for y in range(used):
            head = tab[rows + r * used + y]
            for i, ref in enumerate((q_ref, k_ref, v_ref)):
                light[r * columns + y, i] = col(ref, head)


def post_kernel(rows, tab, light, out):
    columns = light.shape[0] // rows
    used = tab.shape[0] // rows - 1
    for r in range(rows):
        out[:, pl.ds(pl.multiple_of(tab[r] * D, D), D)] = light[r * columns + used]
        for y in range(used):
            at = pl.ds(pl.multiple_of(tab[rows + r * used + y] * D, D), D)
            out[:, at] = light[r * columns + y]


def dot_t(a, b):
    return lax.dot_general(a, b, (((1,), (1,)), ((), ())), preferred_element_type=jnp.float32)


def dot_n(a, b):
    return lax.dot_general(a, b, (((1,), (0,)), ((), ())), preferred_element_type=jnp.float32)


def soft_step(s, v, state):
    top = jnp.max(s, axis=1, keepdims=True)
    if state is None:
        p = jnp.exp2(s - top)
        return top, jnp.sum(p, axis=1, keepdims=True), dot_n(p.astype(jnp.bfloat16), v)
    m, l, acc = state
    new = jnp.maximum(m, top)
    p = jnp.exp2(s - new)
    fix = jnp.exp2(m - new)
    l = l * fix + jnp.sum(p, axis=1, keepdims=True)
    acc = acc * fix + dot_n(p.astype(jnp.bfloat16), v)
    return new, l, acc


def listed(units, lists, counts, total, factor, q_of, k_of, v_of, put):
    def picked(u, turn):
        spots = []
        for j in range(GROUP):
            slot = turn * GROUP + j
            used = slot < counts[u]
            spots.append((used, lists[u * total + jnp.where(used, slot, 0)]))
        return spots

    def scores(u, spots):
        k = jnp.concatenate([k_of(pos) for _, pos in spots], axis=0)
        s = dot_t(q_of(u), k) * factor
        parts = [jnp.where(used, s[:, j * BLOCK : (j + 1) * BLOCK], NEG) for j, (used, _) in enumerate(spots)]
        return jnp.concatenate(parts, axis=1)

    def vals(spots):
        return jnp.concatenate([v_of(pos) for _, pos in spots], axis=0)

    spots = [picked(u, 0) for u in units]
    s = [scores(u, sp) for u, sp in zip(units, spots)]
    states = [soft_step(x, vals(sp), None) for x, sp in zip(s, spots)]
    for u, state in zip(units, states):
        more = (counts[u] + GROUP - 1) // GROUP

        def step(t, st, u=u):
            sp = picked(u, t)
            return soft_step(scores(u, sp), vals(sp), st)

        _, l, acc = lax.fori_loop(1, more, step, state)
        put(u, (acc / l).astype(jnp.bfloat16))


def attend_head(lists, counts, base, q_of, kv, put):
    members, _, n = kv.shape[:3]
    total = members * n
    factor = D ** -0.5 * LOG2E
    low = counts[base]
    for r in range(1, n):
        low = jnp.minimum(low, counts[base + r])

    @pl.when(low == total)
    def dense():
        wide = n // 2

        def part(i, _):
            q = jnp.concatenate([q_of(i * wide + j) for j in range(wide)], axis=0)
            state = None
            for g in range(members):
                k = kv[g, 0].reshape(n * BLOCK, D)
                v = kv[g, 1].reshape(n * BLOCK, D)
                state = soft_step(dot_t(q, k) * factor, v, state)
            _, l, acc = state
            out = (acc / l).astype(jnp.bfloat16)
            for j in range(wide):
                put(i * wide + j, out[j * BLOCK : (j + 1) * BLOCK])
            return 0

        lax.fori_loop(0, n // wide, part, 0)

    @pl.when(low != total)
    def sparse():
        wide = n // 2

        def part(i, _):
            listed(
                [base + i * wide + j for j in range(wide)], lists, counts, total, factor,
                lambda u: q_of(u - base),
                lambda pos: kv[pos // n, 0, pos % n],
                lambda pos: kv[pos // n, 1, pos % n],
                lambda u, x: put(u - base, x),
            )
            return 0

        lax.fori_loop(0, n // wide, part, 0)


def wide_kernel(lists, counts, q_hbm, *refs):
    parts, (o_ref, q_ref, kv, sems) = refs[:-4], refs[-4:]
    spots = []
    for at in (0, kv.shape[0] // 2):
        spots += [kv.at[at], kv.at[at + 1], kv.at[at + 3], kv.at[at + 2, 0], kv.at[at + 2, 1]]
    copies = [pltpu.make_async_copy(part, spot, sems.at[i]) for i, (part, spot) in enumerate(zip(parts, spots))]
    copies.append(pltpu.make_async_copy(q_hbm.at[:, 0], q_ref, sems.at[len(parts)]))
    for copy in copies:
        copy.start()
    for copy in copies:
        copy.wait()

    def put(r, x):
        o_ref[r] = x

    attend_head(lists, counts, 0, lambda r: q_ref[r], kv, put)


def hand_on_kernel(counts, *refs):
    passed, (light, out, sems) = refs[:-3], refs[-3:]

    @pl.when(counts[0] == 0)
    def place():
        copies = [pltpu.make_async_copy(ref, out.at[:, y], sems.at[y]) for y, ref in enumerate(passed)]
        for copy in copies:
            copy.start()
        for copy in copies:
            copy.wait()

    @pl.when(counts[0] > 0)
    def keep():
        out[...] = light[...]


def light_kernel(total, lists, counts, own, other, o_ref, q_ref, kv, sems):
    units = q_ref.shape[0]

    @pl.when(counts[0] > 0)
    def work():
        copies = [
            pltpu.make_async_copy(own.at[:, 0], q_ref, sems.at[0]),
            pltpu.make_async_copy(own.at[:, 1:], kv.at[pl.ds(0, units)], sems.at[1]),
            pltpu.make_async_copy(other.at[:, 1:], kv.at[pl.ds(units, units)], sems.at[2]),
        ]
        for copy in copies:
            copy.start()
        for copy in copies:
            copy.wait()

        def put(u, x):
            o_ref[u] = x

        wide = 16

        def some(i, _):
            listed(
                [i * wide + j for j in range(wide)], lists, counts, total, D ** -0.5 * LOG2E,
                lambda u: q_ref[u], lambda pos: kv[pos, 0], lambda pos: kv[pos, 1], put,
            )
            return 0

        lax.fori_loop(0, units // wide, some, 0)


def local_call(kernel, scalars, inputs, shapes, scratch=(), hbm=0):
    vmem = pl.BlockSpec(memory_space=pltpu.VMEM)
    anywhere = pl.BlockSpec(memory_space=pl.ANY)
    return pl.pallas_call(
        kernel,
        out_shape=[jax.ShapeDtypeStruct(x, jnp.bfloat16) for x in shapes],
        grid_spec=pltpu.PrefetchScalarGridSpec(
            num_scalar_prefetch=len(scalars),
            grid=(),
            in_specs=[anywhere] * hbm + [vmem] * (len(inputs) - hbm),
            out_specs=[vmem] * len(shapes),
            scratch_shapes=list(scratch),
        ),
        compiler_params=pltpu.CompilerParams(vmem_limit_bytes=56 * 2 ** 20),
    )(*scalars, *inputs)


def body(queries, keys, values, key_blocks, block_counts):
    zs = lax.axis_size("z")
    cores = lax.axis_size("core")
    ys = lax.axis_size("split")
    z, c, y = lax.axis_index("z"), lax.axis_index("core"), lax.axis_index("split")
    heads = queries.shape[1] // D
    blocks = key_blocks.shape[1]
    members = cores * ys

    work = jnp.sum(block_counts, axis=1)
    ids = jnp.arange(heads, dtype=jnp.int32)
    ahead = (work[None, :] > work[:, None]) | ((work[None, :] == work[:, None]) & (ids[None, :] < ids[:, None]))
    rank = jnp.sum(ahead.astype(jnp.int32), axis=1)

    def head_at(places):
        return jnp.sum(jnp.where(rank[None, :] == places[:, None], ids[None, :], 0), axis=1)

    used = heads // zs - 1
    rows = jnp.arange(zs, dtype=jnp.int32)
    columns = jnp.arange(used, dtype=jnp.int32)
    table = head_at(jnp.concatenate([rows, ((1 + columns)[None, :] * zs + rows[:, None]).reshape(-1)]))

    def places(lists):
        return lists // members, lists // ys % cores, lists % ys

    wide_head = lax.dynamic_index_in_dim(table, z, keepdims=False)
    wide_ids = rows * members + c * ys + y
    wide_counts = block_counts[wide_head][wide_ids]
    lz, lc, ly = places(key_blocks[wide_head][wide_ids])
    wide_lists = ((lc + c) % cores * ys + (y - ly) % ys) * zs + lz
    light_head = lax.dynamic_index_in_dim(table, zs + z * used + jnp.minimum(y, used - 1), keepdims=False)
    light_ids = jnp.arange(zs * ys, dtype=jnp.int32)
    light_ids = light_ids // ys * members + c * ys + light_ids % ys
    light_counts = jnp.where(y < used, block_counts[light_head][light_ids], 0)
    lz, lc, ly = places(key_blocks[light_head][light_ids])
    light_lists = (lc + c) % cores * (zs * ys) + lz * ys + ly

    wide = local_call(
        wide_prep, [table], [queries, keys, values], [(zs, 3, BLOCK, D)], [pltpu.SemaphoreType.DMA((zs, 3))], hbm=3
    )[0]
    light = local_call(
        functools.partial(light_prep, zs), [table], [queries, keys, values], [(zs * ys, 3, BLOCK, D)]
    )[0]

    def spread(x):
        return lax.all_to_all(x, ("z", "split"), split_axis=0, concat_axis=0, tiled=True)

    def over_cores(x):
        return lax.ppermute(x, "core", [(0, 1), (1, 0)])

    wide = lax.all_to_all(wide, "z", split_axis=0, concat_axis=0, tiled=True)
    wide, light, wide_lists, wide_counts, light_lists, light_counts = lax.optimization_barrier(
        (wide, light, wide_lists, wide_counts, light_lists, light_counts)
    )
    wide_kv = wide[:, 1:].transpose(1, 0, 2, 3)

    def over_y(x, dy):
        return lax.ppermute(x, "split", [(i, (i + dy) % ys) for i in range(ys)])

    before, after = over_y(wide_kv, 1), over_y(wide_kv, -1)
    parts = [wide_kv, before, after, over_y(before[0], 1), over_y(after[1], -1)]
    parts = parts + [over_cores(x) for x in parts]
    light = spread(light)
    wide_out = local_call(
        wide_kernel, [wide_lists.reshape(-1), wide_counts], [wide, *parts], [(zs, BLOCK, D)],
        [
            pltpu.VMEM((zs, BLOCK, D), jnp.bfloat16),
            pltpu.VMEM((members, 2, zs, BLOCK, D), jnp.bfloat16),
            pltpu.SemaphoreType.DMA((len(parts) + 1,)),
        ],
        hbm=len(parts) + 1,
    )[0]
    light, wide_out = lax.optimization_barrier((light, wide_out))
    light_out = local_call(
        functools.partial(light_kernel, blocks), [light_lists.reshape(-1), light_counts],
        [light, over_cores(light)], [(zs * ys, BLOCK, D)],
        [
            pltpu.VMEM((zs * ys, BLOCK, D), jnp.bfloat16),
            pltpu.VMEM((blocks, 2, BLOCK, D), jnp.bfloat16),
            pltpu.SemaphoreType.DMA((3,)),
        ],
        hbm=2,
    )[0]
    passed = [lax.ppermute(wide_out, "split", [(i, used)]) for i in range(used)] + [wide_out]
    light_out = local_call(
        hand_on_kernel, [light_counts], [*passed, light_out.reshape(zs, ys, BLOCK, D)], [(zs, ys, BLOCK, D)],
        [pltpu.SemaphoreType.DMA((ys,))], hbm=ys,
    )[0]
    light_out = spread(light_out.reshape(zs * ys, BLOCK, D))
    return local_call(functools.partial(post_kernel, zs), [table], [light_out], [queries.shape])[0]


def solution(mesh):
    clips, seqs, splits = mesh.devices.shape
    fine = Mesh(mesh.devices.reshape(clips, seqs // 2, 2, splits), ("clip", "z", "core", "split"))
    tokens = P(("clip", "z", "core", "split"), None)
    return jax.shard_map(
        body,
        mesh=fine,
        in_specs=(tokens, tokens, tokens, P("clip", None, None), P("clip", None)),
        out_specs=tokens,
        check_vma=False,
    )
```

```python
import functools

import jax
import jax.numpy as jnp
from jax import lax
from jax.experimental import pallas as pl
from jax.experimental.pallas import tpu as pltpu
from jax.sharding import Mesh, PartitionSpec as P

D = 128
BLOCK = 128
GROUP = 4
NEG = -jnp.inf
LOG2E = 1.4426950408889634


def col(ref, head):
    return ref[:, pl.ds(pl.multiple_of(head * D, D), D)]


def wide_prep(tab, q_ref, k_ref, v_ref, wide, sems):
    copies = []
    for r in range(wide.shape[0]):
        at = pl.ds(pl.multiple_of(tab[r] * D, D), D)
        for i, ref in enumerate((q_ref, k_ref, v_ref)):
            copies.append(pltpu.make_async_copy(ref.at[:, at], wide.at[r, i], sems.at[r, i]))
    for copy in copies:
        copy.start()
    for copy in copies:
        copy.wait()


def light_prep(rows, tab, q_ref, k_ref, v_ref, light):
    columns = light.shape[0] // rows
    used = tab.shape[0] // rows - 1
    for r in range(rows):
        for y in range(used):
            head = tab[rows + r * used + y]
            for i, ref in enumerate((q_ref, k_ref, v_ref)):
                light[r * columns + y, i] = col(ref, head)


def post_kernel(rows, tab, wide, light, out):
    columns = light.shape[0] // rows
    used = tab.shape[0] // rows - 1
    for r in range(rows):
        out[:, pl.ds(pl.multiple_of(tab[r] * D, D), D)] = wide[r]
        for y in range(used):
            at = pl.ds(pl.multiple_of(tab[rows + r * used + y] * D, D), D)
            out[:, at] = light[r * columns + y]


def dot_t(a, b):
    return lax.dot_general(a, b, (((1,), (1,)), ((), ())), preferred_element_type=jnp.float32)


def dot_n(a, b):
    return lax.dot_general(a, b, (((1,), (0,)), ((), ())), preferred_element_type=jnp.float32)


def soft_step(s, v, state):
    top = jnp.max(s, axis=1, keepdims=True)
    if state is None:
        p = jnp.exp2(s - top)
        return top, jnp.sum(p, axis=1, keepdims=True), dot_n(p.astype(jnp.bfloat16), v)
    m, l, acc = state
    new = jnp.maximum(m, top)
    p = jnp.exp2(s - new)
    fix = jnp.exp2(m - new)
    l = l * fix + jnp.sum(p, axis=1, keepdims=True)
    acc = acc * fix + dot_n(p.astype(jnp.bfloat16), v)
    return new, l, acc


def listed(units, lists, counts, total, factor, q_of, k_of, v_of, put):
    def picked(u, turn):
        spots = []
        for j in range(GROUP):
            slot = turn * GROUP + j
            used = slot < counts[u]
            spots.append((used, lists[u * total + jnp.where(used, slot, 0)]))
        return spots

    def scores(u, spots):
        k = jnp.concatenate([k_of(pos) for _, pos in spots], axis=0)
        s = dot_t(q_of(u), k) * factor
        parts = [jnp.where(used, s[:, j * BLOCK : (j + 1) * BLOCK], NEG) for j, (used, _) in enumerate(spots)]
        return jnp.concatenate(parts, axis=1)

    def vals(spots):
        return jnp.concatenate([v_of(pos) for _, pos in spots], axis=0)

    spots = [picked(u, 0) for u in units]
    s = [scores(u, sp) for u, sp in zip(units, spots)]
    states = [soft_step(x, vals(sp), None) for x, sp in zip(s, spots)]
    for u, state in zip(units, states):
        more = (counts[u] + GROUP - 1) // GROUP

        def step(t, st, u=u):
            sp = picked(u, t)
            return soft_step(scores(u, sp), vals(sp), st)

        _, l, acc = lax.fori_loop(1, more, step, state)
        put(u, (acc / l).astype(jnp.bfloat16))


def attend_head(lists, counts, base, q_of, kv, put):
    members, _, n = kv.shape[:3]
    total = members * n
    factor = D ** -0.5 * LOG2E
    low = counts[base]
    for r in range(1, n):
        low = jnp.minimum(low, counts[base + r])

    @pl.when(low == total)
    def dense():
        wide = n // 2

        def part(i, _):
            q = jnp.concatenate([q_of(i * wide + j) for j in range(wide)], axis=0)
            state = None
            for g in range(members):
                k = kv[g, 0].reshape(n * BLOCK, D)
                v = kv[g, 1].reshape(n * BLOCK, D)
                state = soft_step(dot_t(q, k) * factor, v, state)
            _, l, acc = state
            out = (acc / l).astype(jnp.bfloat16)
            for j in range(wide):
                put(i * wide + j, out[j * BLOCK : (j + 1) * BLOCK])
            return 0

        lax.fori_loop(0, n // wide, part, 0)

    @pl.when(low != total)
    def sparse():
        wide = n // 2

        def part(i, _):
            listed(
                [base + i * wide + j for j in range(wide)], lists, counts, total, factor,
                lambda u: q_of(u - base),
                lambda pos: kv[pos // n, 0, pos % n],
                lambda pos: kv[pos // n, 1, pos % n],
                lambda u, x: put(u - base, x),
            )
            return 0

        lax.fori_loop(0, n // wide, part, 0)


def wide_kernel(lists, counts, q_hbm, *refs):
    parts, (o_ref, q_ref, kv, sems) = refs[:-4], refs[-4:]
    spots = []
    for at in (0, kv.shape[0] // 2):
        spots += [kv.at[at], kv.at[at + 1], kv.at[at + 3], kv.at[at + 2, 0], kv.at[at + 2, 1]]
    copies = [pltpu.make_async_copy(part, spot, sems.at[i]) for i, (part, spot) in enumerate(zip(parts, spots))]
    copies.append(pltpu.make_async_copy(q_hbm.at[:, 0], q_ref, sems.at[len(parts)]))
    for copy in copies:
        copy.start()
    for copy in copies:
        copy.wait()

    def put(r, x):
        o_ref[r] = x

    attend_head(lists, counts, 0, lambda r: q_ref[r], kv, put)


def light_kernel(total, lists, counts, own, other, o_ref, q_ref, kv, sems):
    units = q_ref.shape[0]

    @pl.when(counts[0] > 0)
    def work():
        copies = [
            pltpu.make_async_copy(own.at[:, 0], q_ref, sems.at[0]),
            pltpu.make_async_copy(own.at[:, 1:], kv.at[pl.ds(0, units)], sems.at[1]),
            pltpu.make_async_copy(other.at[:, 1:], kv.at[pl.ds(units, units)], sems.at[2]),
        ]
        for copy in copies:
            copy.start()
        for copy in copies:
            copy.wait()

        def put(u, x):
            o_ref[u] = x

        wide = 16

        def some(i, _):
            listed(
                [i * wide + j for j in range(wide)], lists, counts, total, D ** -0.5 * LOG2E,
                lambda u: q_ref[u], lambda pos: kv[pos, 0], lambda pos: kv[pos, 1], put,
            )
            return 0

        lax.fori_loop(0, units // wide, some, 0)


def local_call(kernel, scalars, inputs, shapes, scratch=(), hbm=0):
    vmem = pl.BlockSpec(memory_space=pltpu.VMEM)
    anywhere = pl.BlockSpec(memory_space=pl.ANY)
    return pl.pallas_call(
        kernel,
        out_shape=[jax.ShapeDtypeStruct(x, jnp.bfloat16) for x in shapes],
        grid_spec=pltpu.PrefetchScalarGridSpec(
            num_scalar_prefetch=len(scalars),
            grid=(),
            in_specs=[anywhere] * hbm + [vmem] * (len(inputs) - hbm),
            out_specs=[vmem] * len(shapes),
            scratch_shapes=list(scratch),
        ),
        compiler_params=pltpu.CompilerParams(vmem_limit_bytes=56 * 2 ** 20),
    )(*scalars, *inputs)


def body(queries, keys, values, key_blocks, block_counts):
    zs = lax.axis_size("z")
    cores = lax.axis_size("core")
    ys = lax.axis_size("split")
    z, c, y = lax.axis_index("z"), lax.axis_index("core"), lax.axis_index("split")
    heads = queries.shape[1] // D
    blocks = key_blocks.shape[1]
    members = cores * ys

    work = jnp.sum(block_counts, axis=1)
    ids = jnp.arange(heads, dtype=jnp.int32)
    ahead = (work[None, :] > work[:, None]) | ((work[None, :] == work[:, None]) & (ids[None, :] < ids[:, None]))
    rank = jnp.sum(ahead.astype(jnp.int32), axis=1)

    def head_at(places):
        return jnp.sum(jnp.where(rank[None, :] == places[:, None], ids[None, :], 0), axis=1)

    used = heads // zs - 1
    rows = jnp.arange(zs, dtype=jnp.int32)
    columns = jnp.arange(used, dtype=jnp.int32)
    table = head_at(jnp.concatenate([rows, ((1 + columns)[None, :] * zs + rows[:, None]).reshape(-1)]))

    def places(lists):
        return lists // members, lists // ys % cores, lists % ys

    wide_head = lax.dynamic_index_in_dim(table, z, keepdims=False)
    wide_ids = rows * members + c * ys + y
    wide_counts = block_counts[wide_head][wide_ids]
    lz, lc, ly = places(key_blocks[wide_head][wide_ids])
    wide_lists = ((lc + c) % cores * ys + (y - ly) % ys) * zs + lz
    light_head = lax.dynamic_index_in_dim(table, zs + z * used + jnp.minimum(y, used - 1), keepdims=False)
    light_ids = jnp.arange(zs * ys, dtype=jnp.int32)
    light_ids = light_ids // ys * members + c * ys + light_ids % ys
    light_counts = jnp.where(y < used, block_counts[light_head][light_ids], 0)
    lz, lc, ly = places(key_blocks[light_head][light_ids])
    light_lists = (lc + c) % cores * (zs * ys) + lz * ys + ly

    wide = local_call(
        wide_prep, [table], [queries, keys, values], [(zs, 3, BLOCK, D)], [pltpu.SemaphoreType.DMA((zs, 3))], hbm=3
    )[0]
    light = local_call(
        functools.partial(light_prep, zs), [table], [queries, keys, values], [(zs * ys, 3, BLOCK, D)]
    )[0]

    def spread(x):
        return lax.all_to_all(x, ("z", "split"), split_axis=0, concat_axis=0, tiled=True)

    def over_cores(x):
        return lax.ppermute(x, "core", [(0, 1), (1, 0)])

    wide = lax.all_to_all(wide, "z", split_axis=0, concat_axis=0, tiled=True)
    wide, light, wide_lists, wide_counts, light_lists, light_counts = lax.optimization_barrier(
        (wide, light, wide_lists, wide_counts, light_lists, light_counts)
    )
    wide_kv = wide[:, 1:].transpose(1, 0, 2, 3)

    def over_y(x, dy):
        return lax.ppermute(x, "split", [(i, (i + dy) % ys) for i in range(ys)])

    before, after = over_y(wide_kv, 1), over_y(wide_kv, -1)
    parts = [wide_kv, before, after, over_y(before[0], 1), over_y(after[1], -1)]
    parts = parts + [over_cores(x) for x in parts]
    light = spread(light)
    wide_out = local_call(
        wide_kernel, [wide_lists.reshape(-1), wide_counts], [wide, *parts], [(zs, BLOCK, D)],
        [
            pltpu.VMEM((zs, BLOCK, D), jnp.bfloat16),
            pltpu.VMEM((members, 2, zs, BLOCK, D), jnp.bfloat16),
            pltpu.SemaphoreType.DMA((len(parts) + 1,)),
        ],
        hbm=len(parts) + 1,
    )[0]
    light, wide_out = lax.optimization_barrier((light, wide_out))
    light_out = local_call(
        functools.partial(light_kernel, blocks), [light_lists.reshape(-1), light_counts],
        [light, over_cores(light)], [(zs * ys, BLOCK, D)],
        [
            pltpu.VMEM((zs * ys, BLOCK, D), jnp.bfloat16),
            pltpu.VMEM((blocks, 2, BLOCK, D), jnp.bfloat16),
            pltpu.SemaphoreType.DMA((3,)),
        ],
        hbm=2,
    )[0]
    wide_out = lax.all_to_all(wide_out, "z", split_axis=0, concat_axis=0, tiled=True)
    return local_call(
        functools.partial(post_kernel, zs), [table], [wide_out, spread(light_out)], [queries.shape]
    )[0]


def solution(mesh):
    clips, seqs, splits = mesh.devices.shape
    fine = Mesh(mesh.devices.reshape(clips, seqs // 2, 2, splits), ("clip", "z", "core", "split"))
    tokens = P(("clip", "z", "core", "split"), None)
    return jax.shard_map(
        body,
        mesh=fine,
        in_specs=(tokens, tokens, tokens, P("clip", None, None), P("clip", None)),
        out_specs=tokens,
        check_vma=False,
    )
```

```python
import functools

import jax
import jax.numpy as jnp
from jax import lax
from jax.experimental import pallas as pl
from jax.experimental.pallas import tpu as pltpu
from jax.sharding import Mesh, PartitionSpec as P

D = 128
BLOCK = 128
GROUP = 4
NEG = -jnp.inf
LOG2E = 1.4426950408889634


def col(ref, head):
    return ref[:, pl.ds(pl.multiple_of(head * D, D), D)]


def wide_prep(tab, q_ref, k_ref, v_ref, wide, sems):
    copies = []
    for r in range(wide.shape[0]):
        at = pl.ds(pl.multiple_of(tab[r] * D, D), D)
        for i, ref in enumerate((q_ref, k_ref, v_ref)):
            copies.append(pltpu.make_async_copy(ref.at[:, at], wide.at[r, i], sems.at[r, i]))
    for copy in copies:
        copy.start()
    for copy in copies:
        copy.wait()


def light_prep(rows, tab, q_ref, k_ref, v_ref, light):
    columns = light.shape[0] // rows
    used = tab.shape[0] // rows - 1
    for r in range(rows):
        for y in range(used):
            head = tab[rows + r * used + y]
            for i, ref in enumerate((q_ref, k_ref, v_ref)):
                light[r * columns + y, i] = col(ref, head)


def post_kernel(rows, tab, wide, light, out):
    columns = light.shape[0] // rows
    used = tab.shape[0] // rows - 1
    for r in range(rows):
        out[:, pl.ds(pl.multiple_of(tab[r] * D, D), D)] = wide[r]
        for y in range(used):
            at = pl.ds(pl.multiple_of(tab[rows + r * used + y] * D, D), D)
            out[:, at] = light[r * columns + y]


def dot_t(a, b):
    return lax.dot_general(a, b, (((1,), (1,)), ((), ())), preferred_element_type=jnp.float32)


def dot_n(a, b):
    return lax.dot_general(a, b, (((1,), (0,)), ((), ())), preferred_element_type=jnp.float32)


def soft_step(s, v, state):
    top = jnp.max(s, axis=1, keepdims=True)
    if state is None:
        p = jnp.exp2(s - top)
        return top, jnp.sum(p, axis=1, keepdims=True), dot_n(p.astype(jnp.bfloat16), v)
    m, l, acc = state
    new = jnp.maximum(m, top)
    p = jnp.exp2(s - new)
    fix = jnp.exp2(m - new)
    l = l * fix + jnp.sum(p, axis=1, keepdims=True)
    acc = acc * fix + dot_n(p.astype(jnp.bfloat16), v)
    return new, l, acc


def listed(units, lists, counts, total, factor, q_of, k_of, v_of, put):
    def picked(u, turn):
        spots = []
        for j in range(GROUP):
            slot = turn * GROUP + j
            used = slot < counts[u]
            spots.append((used, lists[u * total + jnp.where(used, slot, 0)]))
        return spots

    def scores(u, spots):
        k = jnp.concatenate([k_of(pos) for _, pos in spots], axis=0)
        s = dot_t(q_of(u), k) * factor
        parts = [jnp.where(used, s[:, j * BLOCK : (j + 1) * BLOCK], NEG) for j, (used, _) in enumerate(spots)]
        return jnp.concatenate(parts, axis=1)

    def vals(spots):
        return jnp.concatenate([v_of(pos) for _, pos in spots], axis=0)

    spots = [picked(u, 0) for u in units]
    s = [scores(u, sp) for u, sp in zip(units, spots)]
    states = [soft_step(x, vals(sp), None) for x, sp in zip(s, spots)]
    for u, state in zip(units, states):
        more = (counts[u] + GROUP - 1) // GROUP

        def step(t, st, u=u):
            sp = picked(u, t)
            return soft_step(scores(u, sp), vals(sp), st)

        _, l, acc = lax.fori_loop(1, more, step, state)
        put(u, (acc / l).astype(jnp.bfloat16))


def attend_head(lists, counts, base, q_of, kv, put):
    members, _, n = kv.shape[:3]
    total = members * n
    factor = D ** -0.5 * LOG2E
    low = counts[base]
    for r in range(1, n):
        low = jnp.minimum(low, counts[base + r])

    @pl.when(low == total)
    def dense():
        wide = n // 2

        def part(i, _):
            q = jnp.concatenate([q_of(i * wide + j) for j in range(wide)], axis=0)
            state = None
            for g in range(members):
                k = kv[g, 0].reshape(n * BLOCK, D)
                v = kv[g, 1].reshape(n * BLOCK, D)
                state = soft_step(dot_t(q, k) * factor, v, state)
            _, l, acc = state
            out = (acc / l).astype(jnp.bfloat16)
            for j in range(wide):
                put(i * wide + j, out[j * BLOCK : (j + 1) * BLOCK])
            return 0

        lax.fori_loop(0, n // wide, part, 0)

    @pl.when(low != total)
    def sparse():
        wide = n // 2

        def part(i, _):
            listed(
                [base + i * wide + j for j in range(wide)], lists, counts, total, factor,
                lambda u: q_of(u - base),
                lambda pos: kv[pos // n, 0, pos % n],
                lambda pos: kv[pos // n, 1, pos % n],
                lambda u, x: put(u - base, x),
            )
            return 0

        lax.fori_loop(0, n // wide, part, 0)


def wide_kernel(lists, counts, q_hbm, *refs):
    parts, (o_ref, q_ref, kv, sems) = refs[:-4], refs[-4:]
    spots = []
    for at in (0, kv.shape[0] // 2):
        spots += [kv.at[at], kv.at[at + 1], kv.at[at + 3], kv.at[at + 2, 0], kv.at[at + 2, 1]]
    copies = [pltpu.make_async_copy(part, spot, sems.at[i]) for i, (part, spot) in enumerate(zip(parts, spots))]
    copies.append(pltpu.make_async_copy(q_hbm.at[:, 0], q_ref, sems.at[len(parts)]))
    for copy in copies:
        copy.start()
    for copy in copies:
        copy.wait()

    def put(r, x):
        o_ref[r] = x

    attend_head(lists, counts, 0, lambda r: q_ref[r], kv, put)


def light_kernel(total, lists, counts, own, other, o_ref, q_ref, kv, sems):
    units = q_ref.shape[0]

    @pl.when(counts[0] > 0)
    def work():
        copies = [
            pltpu.make_async_copy(own.at[:, 0], q_ref, sems.at[0]),
            pltpu.make_async_copy(own.at[:, 1:], kv.at[pl.ds(0, units)], sems.at[1]),
            pltpu.make_async_copy(other.at[:, 1:], kv.at[pl.ds(units, units)], sems.at[2]),
        ]
        for copy in copies:
            copy.start()
        for copy in copies:
            copy.wait()

        def put(u, x):
            o_ref[u] = x

        wide = 16

        def some(i, _):
            listed(
                [i * wide + j for j in range(wide)], lists, counts, total, D ** -0.5 * LOG2E,
                lambda u: q_ref[u], lambda pos: kv[pos, 0], lambda pos: kv[pos, 1], put,
            )
            return 0

        lax.fori_loop(0, units // wide, some, 0)


def local_call(kernel, scalars, inputs, shapes, scratch=(), hbm=0):
    vmem = pl.BlockSpec(memory_space=pltpu.VMEM)
    anywhere = pl.BlockSpec(memory_space=pl.ANY)
    return pl.pallas_call(
        kernel,
        out_shape=[jax.ShapeDtypeStruct(x, jnp.bfloat16) for x in shapes],
        grid_spec=pltpu.PrefetchScalarGridSpec(
            num_scalar_prefetch=len(scalars),
            grid=(),
            in_specs=[anywhere] * hbm + [vmem] * (len(inputs) - hbm),
            out_specs=[vmem] * len(shapes),
            scratch_shapes=list(scratch),
        ),
        compiler_params=pltpu.CompilerParams(vmem_limit_bytes=56 * 2 ** 20),
    )(*scalars, *inputs)


def body(queries, keys, values, key_blocks, block_counts):
    zs = lax.axis_size("z")
    cores = lax.axis_size("core")
    ys = lax.axis_size("split")
    z, c, y = lax.axis_index("z"), lax.axis_index("core"), lax.axis_index("split")
    heads = queries.shape[1] // D
    blocks = key_blocks.shape[1]
    members = cores * ys

    work = jnp.sum(block_counts, axis=1)
    ids = jnp.arange(heads, dtype=jnp.int32)
    ahead = (work[None, :] > work[:, None]) | ((work[None, :] == work[:, None]) & (ids[None, :] < ids[:, None]))
    rank = jnp.sum(ahead.astype(jnp.int32), axis=1)

    def head_at(places):
        return jnp.sum(jnp.where(rank[None, :] == places[:, None], ids[None, :], 0), axis=1)

    used = heads // zs - 1
    rows = jnp.arange(zs, dtype=jnp.int32)
    columns = jnp.arange(used, dtype=jnp.int32)
    table = head_at(jnp.concatenate([rows, ((1 + columns)[None, :] * zs + rows[:, None]).reshape(-1)]))

    def places(lists):
        return lists // members, lists // ys % cores, lists % ys

    wide_head = lax.dynamic_index_in_dim(table, z, keepdims=False)
    wide_ids = rows * members + c * ys + y
    wide_counts = block_counts[wide_head][wide_ids]
    lz, lc, ly = places(key_blocks[wide_head][wide_ids])
    wide_lists = ((lc + c) % cores * ys + (y - ly) % ys) * zs + lz
    light_head = lax.dynamic_index_in_dim(table, zs + z * used + jnp.minimum(y, used - 1), keepdims=False)
    light_ids = jnp.arange(zs * ys, dtype=jnp.int32)
    light_ids = light_ids // ys * members + c * ys + light_ids % ys
    light_counts = jnp.where(y < used, block_counts[light_head][light_ids], 0)
    lz, lc, ly = places(key_blocks[light_head][light_ids])
    light_lists = (lc + c) % cores * (zs * ys) + lz * ys + ly

    wide = local_call(
        wide_prep, [table], [queries, keys, values], [(zs, 3, BLOCK, D)], [pltpu.SemaphoreType.DMA((zs, 3))], hbm=3
    )[0]
    light = local_call(
        functools.partial(light_prep, zs), [table], [queries, keys, values], [(zs * ys, 3, BLOCK, D)]
    )[0]

    def spread(x):
        return lax.all_to_all(x, ("z", "split"), split_axis=0, concat_axis=0, tiled=True)

    def over_cores(x):
        return lax.ppermute(x, "core", [(0, 1), (1, 0)])

    wide = lax.all_to_all(wide, "z", split_axis=0, concat_axis=0, tiled=True)
    wide, light, wide_lists, wide_counts, light_lists, light_counts = lax.optimization_barrier(
        (wide, light, wide_lists.reshape(-1), wide_counts, light_lists.reshape(-1), light_counts)
    )
    wide_kv = wide[:, 1:].transpose(1, 0, 2, 3)

    def over_y(x, dy):
        return lax.ppermute(x, "split", [(i, (i + dy) % ys) for i in range(ys)])

    before, after = over_y(wide_kv, 1), over_y(wide_kv, -1)
    parts = [wide_kv, before, after, over_y(before[0], 1), over_y(after[1], -1)]
    parts = parts + [over_cores(x) for x in parts]
    light = spread(light)
    wide_out = local_call(
        wide_kernel, [wide_lists.reshape(-1), wide_counts], [wide, *parts], [(zs, BLOCK, D)],
        [
            pltpu.VMEM((zs, BLOCK, D), jnp.bfloat16),
            pltpu.VMEM((members, 2, zs, BLOCK, D), jnp.bfloat16),
            pltpu.SemaphoreType.DMA((len(parts) + 1,)),
        ],
        hbm=len(parts) + 1,
    )[0]
    light, wide_out = lax.optimization_barrier((light, wide_out))
    light_out = local_call(
        functools.partial(light_kernel, blocks), [light_lists.reshape(-1), light_counts],
        [light, over_cores(light)], [(zs * ys, BLOCK, D)],
        [
            pltpu.VMEM((zs * ys, BLOCK, D), jnp.bfloat16),
            pltpu.VMEM((blocks, 2, BLOCK, D), jnp.bfloat16),
            pltpu.SemaphoreType.DMA((3,)),
        ],
        hbm=2,
    )[0]
    wide_out = lax.all_to_all(wide_out, "z", split_axis=0, concat_axis=0, tiled=True)
    half = BLOCK // 2
    return pl.pallas_call(
        functools.partial(post_kernel, zs),
        out_shape=jax.ShapeDtypeStruct(queries.shape, jnp.bfloat16),
        grid_spec=pltpu.PrefetchScalarGridSpec(
            num_scalar_prefetch=1,
            grid=(2,),
            in_specs=[
                pl.BlockSpec((zs, half, D), lambda i, *_: (0, i, 0)),
                pl.BlockSpec((zs * ys, half, D), lambda i, *_: (0, i, 0)),
            ],
            out_specs=pl.BlockSpec((half, queries.shape[1]), lambda i, *_: (i, 0)),
        ),
        compiler_params=pltpu.CompilerParams(vmem_limit_bytes=56 * 2 ** 20),
    )(table, wide_out, spread(light_out))


def solution(mesh):
    clips, seqs, splits = mesh.devices.shape
    fine = Mesh(mesh.devices.reshape(clips, seqs // 2, 2, splits), ("clip", "z", "core", "split"))
    tokens = P(("clip", "z", "core", "split"), None)
    return jax.shard_map(
        body,
        mesh=fine,
        in_specs=(tokens, tokens, tokens, P("clip", None, None), P("clip", None)),
        out_specs=tokens,
        check_vma=False,
    )
```
